32 devices in a mesh: group: 2 (over y), expert: 4 (over x, core), tensor: 4 (over z).
Axes of the slice: x: 2, y: 2, z: 4, core: 2. Of those that a mesh axis runs over, the one named last changes fastest.
Arguments:
- tokens: bfloat16 [256, 6144], P(('group', 'expert'), 'tensor'), parts along dimension 0, may hold values from -6 to 6
- route_experts: int32 [256, 2], P(('group', 'expert')), parts along dimension 0, may hold values from 0 to 3, all different within a row; in each aligned block of 32 rows (0 to 31, 32 to 63, ...) at most 20 rows name the same one
- route_weight_values: bfloat16 [256, 2], P(('group', 'expert')), parts along dimension 0, may hold values from 0.099609375 to 0.8984375
- cotangent: bfloat16 [256, 6144], P(('group', 'expert'), 'tensor'), parts along dimension 0, may hold values from -6 to 6
- gate_weight_frozen: bfloat16 [4, 6144, 8192], P('expert', None, 'tensor'), may hold values from -0.078125 to 0.078125
- up_weight_frozen: bfloat16 [4, 6144, 8192], P('expert', None, 'tensor'), may hold values from -0.078125 to 0.078125
- down_weight_frozen: bfloat16 [4, 8192, 6144], P('expert', 'tensor'), may hold values from -0.0625 to 0.0625
- entry_input_maps: bfloat16 [8, 2, 6144, 16], P('group', None, 'tensor'), parts along dimension 0, may hold values from -0.078125 to 0.078125
- entry_output_maps: bfloat16 [8, 2, 16, 8192], P(('group', 'expert'), None, None, 'tensor'), parts along dimension 0, may hold values from -0.29882812 to 0.29882812
- down_input_maps: bfloat16 [8, 8192, 16], P(('group', 'expert'), 'tensor'), parts along dimension 0, may hold values from -0.0625 to 0.0625
- down_output_maps: bfloat16 [8, 16, 6144], P('group', None, 'tensor'), parts along dimension 0, may hold values from -0.29882812 to 0.29882812
Outputs:
- mixed: bfloat16 [256, 6144], P(('group', 'expert'), 'tensor'), parts along dimension 0
- grad_tokens: bfloat16 [256, 6144], P(('group', 'expert'), 'tensor'), parts along dimension 0
- entry_inmaps_gradient: float32 [8, 2, 6144, 16], P('group', None, ('expert', 'tensor')), parts along dimension 0
- entry_outmaps_gradient: float32 [8, 2, 16, 8192], P(('group', 'expert'), None, None, 'tensor'), parts along dimension 0
- down_inmaps_gradient: float32 [8, 8192, 16], P(('group', 'expert'), 'tensor'), parts along dimension 0
- down_outmaps_gradient: float32 [8, 16, 6144], P('group', None, ('expert', 'tensor')), parts along dimension 0
The draws below stay inside these ranges and needn't reach their ends.
There are 2 independent parts, one for each index of `group`. The reference program is written for one: setup_inputs(seed, part) draws one part's arguments, and reference() takes and returns one part's arrays. A program takes and returns all parts, laid end to end along the dimension named above; an argument that names none is the same for every part. Nothing has to cross between parts.
Inputs may be any that keep to these rules, and one draw needn't show every extreme that they name: `route_experts`: each token names 2 different experts. Among the tokens of one index of expert (aligned blocks of 32 tokens) no expert is named by more than 20 of them, and in every draw some block has an expert named by exactly 20.
All inputs are finite; a program needn't handle non-finite values.
Results may differ from the reference program's by a relative error of at most 0.006.
Values may be sent and summed in bfloat16 or wider, within the bound.
A program may use at most 192 MiB of HBM per device.

```python
import math
import jax
import jax.numpy as jnp
import numpy as np
from jax import lax

MODEL_DIM = 6144
HIDDEN_UNITS = 8192
LOCAL_EXPERTS = 4
TOP = 2
ADAPTER_RANK = 16
TOK_DEV = 32
MOST = 20
SLICE_TOTAL = 4
SLICE_UNITS = 8192
TOKENS = 128
N_EXPERT = 4


def block_levels(stream_key, extent, pieces, smallest, top_value):
    gain, own = 1.0, jax.random.fold_in(stream_key, 6)
    for dim, parts in pieces:
        draws = jnp.exp(jax.random.uniform(jax.random.fold_in(own, dim), (parts,), jnp.float32, smallest / len(pieces), top_value / len(pieces)))
        gain = gain * jnp.repeat(draws, extent[dim] // parts).reshape([-1 if axis == dim else 1 for axis in range(len(extent))])
    return gain


def assign_block(key, own, number, rows, number_of, top, reach, slope):
    ranking = jax.random.permutation(key, number_of)
    crowded, ordinary = portions_of(number_of, rows * top, reach, slope, True), portions_of(number_of, rows * top, reach, slope, False)
    places = jnp.arange(number_of)

    def named(lengths, offset_by):
        used = int((lengths > 0).sum())
        fixed = max(1, used // 4)
        shifted = fixed + (places - fixed + offset_by * (used - fixed)) % max(1, number_of - fixed)
        return jnp.zeros((number_of,), jnp.int32).at[ranking[jnp.where(places < fixed, places, shifted)]].set(jnp.asarray(lengths, jnp.int32))

    lengths = jnp.where(number % 4 == 0, named(crowded, number // 4), named(ordinary, number - number // 4 - 1))
    mixed = jax.random.permutation(jax.random.fold_in(own, 3), number_of)
    source_of, taker = mixed[0:number_of // 2 * 2:2], mixed[1:number_of // 2 * 2:2]
    slack = jnp.minimum(lengths[source_of] - 1, reach - lengths[taker]) // 2
    slack = jnp.where((source_of == ranking[0]) | (taker == ranking[0]) | (lengths[taker] == 0), 0, jnp.maximum(slack, 0))
    shifted = jax.random.randint(jax.random.fold_in(own, 4), (number_of // 2,), 0, 1 << 20) % (slack + 1)
    lengths = lengths.at[source_of].add(-shifted).at[taker].add(shifted)
    members = jnp.searchsorted(jnp.cumsum(lengths), jnp.arange(rows * top), side="right").astype(jnp.int32)
    grid = members.reshape(top, rows).T
    grid = grid[jax.random.permutation(jax.random.fold_in(own, 1), rows)]
    offset_by = jax.random.randint(jax.random.fold_in(own, 2), (rows, 1), 0, top)
    return jnp.take_along_axis(grid, (jnp.arange(top)[None, :] + offset_by) % top, axis=1)


def portions_of(number_of, total, reach, skew, full):
    weights = [(1 << 20) // math.isqrt(standing ** skew) + 1 for standing in range(1, number_of + 1)]
    largest = reach if full else min(reach, max(-(-total // number_of), total * weights[0] // sum(weights)))
    least = 1 if total - largest >= number_of - 1 else 0
    counts, rest = [largest] + [least] * (number_of - 1), total - largest - least * (number_of - 1)
    while rest > 0:
        candidates = [i for i in range(1, number_of) if counts[i] < largest] or [i for i in range(1, number_of) if counts[i] < reach]
        pool, remaining = sum([weights[i] for i in candidates]), rest
        for i in candidates:
            more = min(reach - counts[i], max(1, remaining * weights[i] // pool), rest)
            counts[i] = counts[i] + more
            rest = rest - more
    return np.array(counts)


def centred(own_key, shape, spread, most, split=(), kind=jnp.bfloat16):
    drawn = spread * jax.random.normal(own_key, shape, jnp.float32)
    if split:
        drawn = drawn * block_levels(own_key, shape, split, -0.22, 0.18)
    return jnp.clip(drawn, -most, most).astype(kind)


def setup_inputs(seed: int = 0, part: int = 0) -> dict:
    seeds = jax.random.split(jax.random.key(seed), 12)
    own_keys = jax.random.split(jax.random.fold_in(seeds[11], part), 12)
    tokens = centred(own_keys[0], (TOKENS, MODEL_DIM), 1.0, 6.0, ((0, 4), (1, 4)))
    route_experts_keys = jax.random.split(jax.random.fold_in(own_keys[1], 1), TOKENS // TOK_DEV)
    route_experts_turns = jax.random.permutation(jax.random.fold_in(own_keys[1], 3), TOKENS // TOK_DEV)
    route_experts = jax.vmap(lambda own, number: assign_block(jax.random.fold_in(own_keys[1], 2), own, number, TOK_DEV, LOCAL_EXPERTS, TOP, MOST, 2))(route_experts_keys, route_experts_turns).reshape((TOKENS, TOP))
    route_weight_values = jnp.clip(0.099609375 + 0.7988281 * jax.random.uniform(own_keys[2], (TOKENS, TOP), jnp.float32) ** block_levels(own_keys[2], (TOKENS, TOP), ((0, 4),), -0.2, 0.2), 0.099609375, 0.8984375).astype(jnp.bfloat16)
    cotangent = centred(own_keys[3], (TOKENS, MODEL_DIM), 1.0, 6.0, ((0, 4), (1, 4)))
    gate_weight_frozen = centred(seeds[4], (SLICE_TOTAL, MODEL_DIM, SLICE_UNITS), MODEL_DIM ** -0.5, 0.078125, ((0, 4), (2, 4)))
    up_weight_frozen = centred(seeds[5], (SLICE_TOTAL, MODEL_DIM, SLICE_UNITS), MODEL_DIM ** -0.5, 0.078125, ((0, 4), (2, 4)))
    down_weight_frozen = centred(seeds[6], (SLICE_TOTAL, SLICE_UNITS, MODEL_DIM), HIDDEN_UNITS ** -0.5, 0.0625, ((0, 4), (1, 4)))
    entry_input_maps = centred(own_keys[7], (LOCAL_EXPERTS, 2, MODEL_DIM, ADAPTER_RANK), MODEL_DIM ** -0.5, 0.078125, ((2, 4),))
    entry_output_maps = centred(own_keys[8], (SLICE_TOTAL, 2, ADAPTER_RANK, SLICE_UNITS), 0.05, 0.29882812, ((0, 4), (3, 4)))
    down_input_maps = centred(own_keys[9], (SLICE_TOTAL, SLICE_UNITS, ADAPTER_RANK), HIDDEN_UNITS ** -0.5, 0.0625, ((0, 4), (1, 4)))
    down_output_maps = centred(own_keys[10], (LOCAL_EXPERTS, ADAPTER_RANK, MODEL_DIM), 0.05, 0.29882812, ((2, 4),))
    return {"tokens": tokens, "route_experts": route_experts, "route_weight_values": route_weight_values, "cotangent": cotangent, "gate_weight_frozen": gate_weight_frozen, "up_weight_frozen": up_weight_frozen, "down_weight_frozen": down_weight_frozen, "entry_input_maps": entry_input_maps, "entry_output_maps": entry_output_maps, "down_input_maps": down_input_maps, "down_output_maps": down_output_maps}


adapter_scale = 2.0
exact_precision = lax.Precision.HIGHEST


def expert_forward_step(expert_token_rows, expert_gradient_rows, expert_gate_values, gate_weight_slices, up_weight_slices, down_weight_slices, adapter_a_in, entry_adapter_outmaps, down_adapter_inmaps, adapter_b_down):
    narrow_gate = jnp.dot(expert_token_rows, adapter_a_in[0], preferred_element_type=jnp.float32).astype(jnp.bfloat16)
    narrow_up = jnp.dot(expert_token_rows, adapter_a_in[1], preferred_element_type=jnp.float32).astype(jnp.bfloat16)
    gate_preactivation = jnp.dot(expert_token_rows, gate_weight_slices, preferred_element_type=jnp.float32) + adapter_scale * jnp.dot(narrow_gate, entry_adapter_outmaps[0], preferred_element_type=jnp.float32)
    up_preactivation = jnp.dot(expert_token_rows, up_weight_slices, preferred_element_type=jnp.float32) + adapter_scale * jnp.dot(narrow_up, entry_adapter_outmaps[1], preferred_element_type=jnp.float32)
    sigmoid_gate = jax.nn.sigmoid(gate_preactivation)
    silu_gate = gate_preactivation * sigmoid_gate
    hidden_state = (silu_gate * up_preactivation).astype(jnp.bfloat16)
    narrow_down = jnp.dot(hidden_state, down_adapter_inmaps, preferred_element_type=jnp.float32)
    down_output_maps_spread = adapter_b_down.astype(jnp.float32)
    expert_output_rows = jnp.dot(hidden_state, down_weight_slices, preferred_element_type=jnp.float32) + adapter_scale * jnp.dot(narrow_down, down_output_maps_spread, precision=exact_precision)
    weighted = expert_gate_values * expert_output_rows
    output_gradient = (expert_gate_values * expert_gradient_rows.astype(jnp.float32)).astype(jnp.bfloat16)
    narrow_gradient = jnp.dot(output_gradient, adapter_b_down.T, preferred_element_type=jnp.float32)
    hidden_gradient = jnp.dot(output_gradient, down_weight_slices.T, preferred_element_type=jnp.float32) + adapter_scale * jnp.dot(narrow_gradient, down_adapter_inmaps.astype(jnp.float32).T, precision=exact_precision)
    down_inmaps_gradient = adapter_scale * jnp.dot(hidden_state.astype(jnp.float32).T, narrow_gradient, precision=exact_precision)
    down_outmaps_gradient = adapter_scale * jnp.dot(narrow_down.T, output_gradient.astype(jnp.float32), precision=exact_precision)
    gate_gradient = (hidden_gradient * up_preactivation * sigmoid_gate * (1.0 + gate_preactivation * (1.0 - sigmoid_gate))).astype(jnp.bfloat16)
    up_gradient = (hidden_gradient * silu_gate).astype(jnp.bfloat16)
    reverse_gate_step = jnp.dot(gate_gradient, entry_adapter_outmaps[0].T, preferred_element_type=jnp.float32)
    reverse_up_step = jnp.dot(up_gradient, entry_adapter_outmaps[1].T, preferred_element_type=jnp.float32)
    entry_outmaps_gradient = adapter_scale * jnp.stack([jnp.dot(narrow_gate.T, gate_gradient, preferred_element_type=jnp.float32), jnp.dot(narrow_up.T, up_gradient, preferred_element_type=jnp.float32)])
    token_rows_spread = expert_token_rows.astype(jnp.float32)
    entry_inmaps_gradient = adapter_scale * jnp.stack([jnp.dot(token_rows_spread.T, reverse_gate_step, precision=exact_precision), jnp.dot(token_rows_spread.T, reverse_up_step, precision=exact_precision)])
    entry_input_maps_spread = adapter_a_in.astype(jnp.float32)
    input_gradient = jnp.dot(gate_gradient, gate_weight_slices.T, preferred_element_type=jnp.float32) + jnp.dot(up_gradient, up_weight_slices.T, preferred_element_type=jnp.float32)
    input_gradient = input_gradient + adapter_scale * (jnp.dot(reverse_gate_step, entry_input_maps_spread[0].T, precision=exact_precision) + jnp.dot(reverse_up_step, entry_input_maps_spread[1].T, precision=exact_precision))
    return weighted, input_gradient, entry_inmaps_gradient, entry_outmaps_gradient, down_inmaps_gradient, down_outmaps_gradient


def reference(tokens, route_experts, route_weight_values, cotangent, gate_weight_frozen, up_weight_frozen, down_weight_frozen, entry_input_maps, entry_output_maps, down_input_maps, down_output_maps):
    copy_count = N_EXPERT // LOCAL_EXPERTS
    capacity = N_EXPERT * MOST
    flat_ids = route_experts.reshape(-1)
    flat_gates = route_weight_values.reshape(-1)
    route_order = jnp.arange(TOKENS * TOP, dtype=jnp.int32)
    mixed = jnp.zeros((TOKENS, MODEL_DIM), jnp.float32)
    grad_tokens = jnp.zeros((TOKENS, MODEL_DIM), jnp.float32)
    list_a_in, list_b_in, list_a_down, list_b_down = [], [], [], []
    for expert_index in range(LOCAL_EXPERTS):
        sort_keys = jnp.where(flat_ids == expert_index, route_order, TOKENS * TOP).astype(jnp.int32)
        picked = jnp.argsort(sort_keys)[:capacity].astype(jnp.int32)
        is_routed = flat_ids[picked] == expert_index
        row_tokens = (picked // TOP).astype(jnp.int32)
        expert_token_rows = tokens[row_tokens]
        expert_gradient_rows = cotangent[row_tokens]
        expert_gate_values = jnp.where(is_routed, flat_gates[picked].astype(jnp.float32), 0.0)[:, None]
        starting_slice = expert_index * copy_count
        ending_slice = starting_slice + copy_count
        gate_matrix_whole = jnp.transpose(gate_weight_frozen[starting_slice:ending_slice], (1, 0, 2)).reshape(MODEL_DIM, HIDDEN_UNITS)
        up_matrix_whole = jnp.transpose(up_weight_frozen[starting_slice:ending_slice], (1, 0, 2)).reshape(MODEL_DIM, HIDDEN_UNITS)
        down_matrix_whole = down_weight_frozen[starting_slice:ending_slice].reshape(HIDDEN_UNITS, MODEL_DIM)
        entry_output_maps_whole = jnp.transpose(entry_output_maps[starting_slice:ending_slice], (1, 2, 0, 3)).reshape(2, ADAPTER_RANK, HIDDEN_UNITS)
        down_input_maps_whole = down_input_maps[starting_slice:ending_slice].reshape(HIDDEN_UNITS, ADAPTER_RANK)
        step_results = expert_forward_step(expert_token_rows, expert_gradient_rows, expert_gate_values, gate_matrix_whole, up_matrix_whole, down_matrix_whole, entry_input_maps[expert_index], entry_output_maps_whole, down_input_maps_whole, down_output_maps[expert_index])
        weighted, input_gradient, entry_inmaps_gradient, entry_outmaps_gradient, down_inmaps_gradient, down_outmaps_gradient = step_results
        mixed = mixed.at[row_tokens].add(weighted)
        grad_tokens = grad_tokens.at[row_tokens].add(input_gradient)
        list_a_in.append(entry_inmaps_gradient)
        list_b_in.append(jnp.transpose(entry_outmaps_gradient.reshape(2, ADAPTER_RANK, copy_count, SLICE_UNITS), (2, 0, 1, 3)))
        list_a_down.append(down_inmaps_gradient.reshape(copy_count, SLICE_UNITS, ADAPTER_RANK))
        list_b_down.append(down_outmaps_gradient)
    return (mixed.astype(jnp.bfloat16), grad_tokens.astype(jnp.bfloat16), jnp.stack(list_a_in), jnp.concatenate(list_b_in, axis=0), jnp.concatenate(list_a_down, axis=0), jnp.stack(list_b_down))
```

```python
import functools

import jax
import jax.numpy as jnp
from jax import lax
from jax.experimental import pallas as pl
from jax.experimental.pallas import tpu as pltpu
from jax.sharding import PartitionSpec as P

MOST = 20


adapter_scale = 2.0
exact_precision = lax.Precision.HIGHEST


def expert_forward_step(
    expert_token_rows,
    expert_gradient_rows,
    expert_gate_values,
    gate_weight_slices,
    up_weight_slices,
    down_weight_slices,
    adapter_a_in,
    entry_adapter_outmaps,
    down_adapter_inmaps,
    adapter_b_down,
):
    narrow_gate = jnp.dot(
        expert_token_rows, adapter_a_in[0], preferred_element_type=jnp.float32
    ).astype(jnp.bfloat16)
    narrow_up = jnp.dot(
        expert_token_rows, adapter_a_in[1], preferred_element_type=jnp.float32
    ).astype(jnp.bfloat16)
    gate_preactivation = jnp.dot(
        expert_token_rows, gate_weight_slices, preferred_element_type=jnp.float32
    ) + adapter_scale * jnp.dot(
        narrow_gate, entry_adapter_outmaps[0], preferred_element_type=jnp.float32
    )
    up_preactivation = jnp.dot(
        expert_token_rows, up_weight_slices, preferred_element_type=jnp.float32
    ) + adapter_scale * jnp.dot(
        narrow_up, entry_adapter_outmaps[1], preferred_element_type=jnp.float32
    )
    sigmoid_gate = jax.nn.sigmoid(gate_preactivation)
    silu_gate = gate_preactivation * sigmoid_gate
    hidden_state = (silu_gate * up_preactivation).astype(jnp.bfloat16)
    narrow_down = jnp.dot(hidden_state, down_adapter_inmaps, preferred_element_type=jnp.float32)
    down_output_maps_spread = adapter_b_down.astype(jnp.float32)
    expert_output_rows = jnp.dot(
        hidden_state, down_weight_slices, preferred_element_type=jnp.float32
    ) + adapter_scale * jnp.dot(narrow_down, down_output_maps_spread, precision=exact_precision)
    weighted = expert_gate_values * expert_output_rows
    output_gradient = (expert_gate_values * expert_gradient_rows.astype(jnp.float32)).astype(
        jnp.bfloat16
    )
    narrow_gradient = jnp.dot(output_gradient, adapter_b_down.T, preferred_element_type=jnp.float32)
    hidden_gradient = jnp.dot(
        output_gradient, down_weight_slices.T, preferred_element_type=jnp.float32
    ) + adapter_scale * jnp.dot(
        narrow_gradient, down_adapter_inmaps.astype(jnp.float32).T, precision=exact_precision
    )
    down_inmaps_gradient = adapter_scale * jnp.dot(
        hidden_state.astype(jnp.float32).T, narrow_gradient, precision=exact_precision
    )
    down_outmaps_gradient = adapter_scale * jnp.dot(
        narrow_down.T, output_gradient.astype(jnp.float32), precision=exact_precision
    )
    gate_gradient = (
        hidden_gradient
        * up_preactivation
        * sigmoid_gate
        * (1.0 + gate_preactivation * (1.0 - sigmoid_gate))
    ).astype(jnp.bfloat16)
    up_gradient = (hidden_gradient * silu_gate).astype(jnp.bfloat16)
    reverse_gate_step = jnp.dot(
        gate_gradient, entry_adapter_outmaps[0].T, preferred_element_type=jnp.float32
    )
    reverse_up_step = jnp.dot(
        up_gradient, entry_adapter_outmaps[1].T, preferred_element_type=jnp.float32
    )
    entry_outmaps_gradient = adapter_scale * jnp.stack(
        [
            jnp.dot(narrow_gate.T, gate_gradient, preferred_element_type=jnp.float32),
            jnp.dot(narrow_up.T, up_gradient, preferred_element_type=jnp.float32),
        ]
    )
    token_rows_spread = expert_token_rows.astype(jnp.float32)
    entry_inmaps_gradient = adapter_scale * jnp.stack(
        [
            jnp.dot(token_rows_spread.T, reverse_gate_step, precision=exact_precision),
            jnp.dot(token_rows_spread.T, reverse_up_step, precision=exact_precision),
        ]
    )
    entry_input_maps_spread = adapter_a_in.astype(jnp.float32)
    input_gradient = jnp.dot(
        gate_gradient, gate_weight_slices.T, preferred_element_type=jnp.float32
    ) + jnp.dot(up_gradient, up_weight_slices.T, preferred_element_type=jnp.float32)
    input_gradient = input_gradient + adapter_scale * (
        jnp.dot(reverse_gate_step, entry_input_maps_spread[0].T, precision=exact_precision)
        + jnp.dot(reverse_up_step, entry_input_maps_spread[1].T, precision=exact_precision)
    )
    return (
        weighted,
        input_gradient,
        entry_inmaps_gradient,
        entry_outmaps_gradient,
        down_inmaps_gradient,
        down_outmaps_gradient,
    )


def route_positions(route_experts, expert_number):
    flat_ids = route_experts.reshape(-1)
    expert_labels = jnp.arange(expert_number, dtype=jnp.int32)
    one_hot = (flat_ids[:, None] == expert_labels[None, :]).astype(jnp.int32)
    earlier = jnp.cumsum(one_hot, axis=0) - one_hot
    return jnp.sum(earlier * one_hot, axis=1)


def spread_slots(rows, expert_number, capacity, copy_count):
    return jnp.repeat(rows.reshape((expert_number, capacity) + rows.shape[1:]), copy_count, axis=0)


def collect_rows(back, token_hits, expert_number, copy_count, capacity):
    row_width = back.shape[2]
    merged = jnp.sum(back.reshape(expert_number, copy_count, capacity, row_width), axis=1).reshape(
        expert_number * capacity, row_width
    )
    return jnp.dot(token_hits.T, merged, precision=exact_precision)


def local(
    tokens,
    route_experts,
    route_weight_values,
    cotangent,
    gate_weight_frozen,
    up_weight_frozen,
    down_weight_frozen,
    entry_input_maps,
    entry_output_maps,
    down_input_maps,
    down_output_maps,
):
    tok_rows = tokens.shape[0]
    expert_number = entry_input_maps.shape[0]
    adapter_rank_count = entry_input_maps.shape[3]
    route_count = route_experts.shape[1]
    owner_count = lax.axis_size("expert")
    tensor_count = lax.axis_size("tensor")
    model_width = tokens.shape[1] * tensor_count
    copy_count = owner_count // expert_number
    capacity = MOST
    flat_ids = route_experts.reshape(-1)
    position = route_positions(route_experts, expert_number)
    slot_of = flat_ids * capacity + position
    slot_ids = jnp.arange(expert_number * capacity, dtype=jnp.int32)
    chosen = slot_ids[:, None] == slot_of[None, :]
    pick_route = chosen.astype(jnp.bfloat16)
    hit_counts = jnp.sum(
        chosen.reshape(expert_number * capacity, tok_rows, route_count).astype(jnp.int32), axis=2
    )
    pick_token = hit_counts.astype(jnp.bfloat16)
    token_hits = hit_counts.astype(jnp.float32)
    send_gates = jnp.dot(
        pick_route, route_weight_values.reshape(-1), preferred_element_type=jnp.float32
    ).astype(jnp.bfloat16)
    send_gates = spread_slots(send_gates, expert_number, capacity, copy_count)
    full_tokens, full_grads = (
        lax.all_gather(tokens, "tensor", axis=1, tiled=True),
        lax.all_gather(cotangent, "tensor", axis=1, tiled=True),
    )
    send_tokens = spread_slots(
        jnp.dot(pick_token, full_tokens, preferred_element_type=jnp.float32).astype(jnp.bfloat16),
        expert_number,
        capacity,
        copy_count,
    )
    send_grads = spread_slots(
        jnp.dot(pick_token, full_grads, preferred_element_type=jnp.float32).astype(jnp.bfloat16),
        expert_number,
        capacity,
        copy_count,
    )
    got_tokens, got_grads, got_gates = (
        lax.all_to_all(send_tokens, "expert", split_axis=0, concat_axis=0, tiled=True),
        lax.all_to_all(send_grads, "expert", split_axis=0, concat_axis=0, tiled=True),
        lax.all_to_all(send_gates, "expert", split_axis=0, concat_axis=0, tiled=True),
    )
    holder_index = lax.axis_index("expert") // copy_count
    entry_input_maps_local = lax.dynamic_index_in_dim(
        entry_input_maps, holder_index, 0, keepdims=False
    )
    down_output_maps_local = lax.dynamic_index_in_dim(
        down_output_maps, holder_index, 0, keepdims=False
    )
    a_in_full, b_down_full = (
        lax.all_gather(entry_input_maps_local, "tensor", axis=1, tiled=True),
        lax.all_gather(down_output_maps_local, "tensor", axis=1, tiled=True),
    )
    expert_token_rows = got_tokens.reshape(-1, model_width)
    expert_gradient_rows = got_grads.reshape(-1, model_width)
    expert_gate_values = got_gates.reshape(-1).astype(jnp.float32)[:, None]
    step_results = expert_forward_step(
        expert_token_rows,
        expert_gradient_rows,
        expert_gate_values,
        gate_weight_frozen[0],
        up_weight_frozen[0],
        down_weight_frozen[0],
        a_in_full,
        entry_output_maps[0],
        down_input_maps[0],
        b_down_full,
    )
    (
        weighted,
        input_gradient,
        entry_inmaps_gradient,
        entry_outmaps_gradient,
        down_inmaps_gradient,
        down_outmaps_gradient,
    ) = step_results
    weighted = weighted.reshape(owner_count, capacity, model_width)
    input_gradient = input_gradient.reshape(owner_count, capacity, model_width)
    back_out, back_grad = (
        lax.all_to_all(weighted, "expert", split_axis=0, concat_axis=0, tiled=True),
        lax.all_to_all(input_gradient, "expert", split_axis=0, concat_axis=0, tiled=True),
    )
    token_out = collect_rows(back_out, token_hits, expert_number, copy_count, capacity)
    token_grad = collect_rows(back_grad, token_hits, expert_number, copy_count, capacity)
    total_out, total_grad = (
        lax.psum_scatter(token_out, "tensor", scatter_dimension=1, tiled=True),
        lax.psum_scatter(token_grad, "tensor", scatter_dimension=1, tiled=True),
    )
    table_a_in = jnp.zeros((expert_number, 2, model_width, adapter_rank_count), jnp.float32)
    table_a_in = lax.dynamic_update_index_in_dim(table_a_in, entry_inmaps_gradient, holder_index, 0)
    table_b_down = jnp.zeros((expert_number, adapter_rank_count, model_width), jnp.float32)
    table_b_down = lax.dynamic_update_index_in_dim(
        table_b_down, down_outmaps_gradient, holder_index, 0
    )
    summed_a_in, summed_b_down = (
        lax.psum_scatter(table_a_in, ("expert", "tensor"), scatter_dimension=2, tiled=True),
        lax.psum_scatter(table_b_down, ("expert", "tensor"), scatter_dimension=2, tiled=True),
    )
    return (
        total_out.astype(jnp.bfloat16),
        total_grad.astype(jnp.bfloat16),
        summed_a_in,
        entry_outmaps_gradient[None],
        down_inmaps_gradient[None],
        summed_b_down,
    )


BF = jnp.bfloat16
F32 = jnp.float32
MESH = pl.DeviceIdType.MESH
BLOCK = 256
SLOTS = 4


def dot_nn(a, b):
    return jnp.dot(a, b, preferred_element_type=F32)


def dot_nt(a, b):
    return lax.dot_general(a, b, (((1,), (1,)), ((), ())), preferred_element_type=F32)


def dot_exact(a, b):
    return jnp.dot(a, b, preferred_element_type=F32, precision=exact_precision)


def fused_kernel(
    n_tensor,
    tok_ref, cot_ref, gates_ref, at_ref, bd_ref, bin_ref, adt_ref, wg_ref, wu_ref, wd_ref,
    mixed_ref, grad_ref, ein_ref, eout_ref, din_ref, dout_ref,
    xy, small, gmat, sel_ref, selt_ref, acc, tacc, tz, ts, te, tvz, tvzt,
    wg_buf, wu_buf, wd_buf, s1, r1, s2, r2, s3, r3, keep,
    wsem, gz_s, gz_r, gx_s, gx_r, gs_s, gs_r, gf_s, gf_r,
    tz_s, tz_r, te_s, te_r, c1_s, c1_r, c2_s, c2_r, c3_s, c3_r,
):
    e = lax.axis_index("expert")
    t = lax.axis_index("tensor")
    n = n_tensor
    tr, f = tok_ref.shape
    rows, width = gmat.shape
    units = adt_ref.shape[1]
    blocks = units // BLOCK
    xi, ci = e // 2, e % 2
    sib = 2 * xi + (1 - ci)
    xc = 2 * (1 - xi) + ci
    diag = 2 * (1 - xi) + (1 - ci)

    def z_to(i):
        return lax.rem(t + i, n)

    def z_from(i):
        return lax.rem(t - i + n, n)

    def remote(src, dst, ss, rs, pe, pt):
        return pltpu.make_async_remote_copy(
            src_ref=src, dst_ref=dst, send_sem=ss, recv_sem=rs,
            device_id={"expert": pe, "tensor": pt}, device_id_type=MESH,
        )

    def weight_copies(j, slot):
        cols = pl.ds(pl.multiple_of(j * BLOCK, BLOCK), BLOCK)
        return (
            pltpu.make_async_copy(wg_ref.at[0, :, cols], wg_buf.at[slot], wsem.at[0, slot]),
            pltpu.make_async_copy(wu_ref.at[0, :, cols], wu_buf.at[slot], wsem.at[1, slot]),
            pltpu.make_async_copy(wd_ref.at[0, cols, :], wd_buf.at[slot], wsem.at[2, slot]),
        )

    barrier = pltpu.get_barrier_semaphore()
    for i in range(1, n):
        pl.semaphore_signal(
            barrier, inc=1, device_id={"expert": e, "tensor": z_to(i)}, device_id_type=MESH
        )
    for j in range(1, 4):
        pl.semaphore_signal(
            barrier, inc=1, device_id={"expert": lax.rem(e + j, 4), "tensor": t},
            device_id_type=MESH,
        )

    def row_ds(o):
        return pl.ds(pl.multiple_of(o * tr, tr), tr)

    def col_ds(q):
        return pl.ds(pl.multiple_of(q * f, f), f)

    def part(k, oe, ot):
        if k == 0:
            return xy.at[:, row_ds(oe), col_ds(ot)]
        return small.at[ot, row_ds(oe), :]

    xy[0, row_ds(e), col_ds(t)] = tok_ref[...]
    xy[1, row_ds(e), col_ds(t)] = cot_ref[...]
    pl.semaphore_wait(barrier, n - 1 + 3)

    sends = []

    def start(copy):
        copy.start()
        sends.append(copy)

    def z_copy(k, i):
        return remote(part(k, e, t), part(k, e, t), gz_s.at[k, i], gz_r.at[k, i], e, z_to(i))

    def x_copy(k, i):
        b = part(k, e, z_from(i))
        return remote(b, b, gx_s.at[k, i], gx_r.at[k, i], xc, t)

    def sib_copy(k, i):
        b = part(k, e, z_from(i))
        return remote(b, b, gs_s.at[k, i], gs_r.at[k, i], sib, t)

    def fwd_copy(k, i):
        b = part(k, xc, z_from(i))
        return remote(b, b, gf_s.at[k, i], gf_r.at[k, i], sib, t)

    def landed(k, oe, ot, rs):
        b = part(k, oe, ot)
        remote(b, b, rs, rs, sib, t).wait_recv()

    for i in range(1, n):
        start(z_copy(0, i))
    start(x_copy(0, 0))
    start(sib_copy(0, 0))
    for j in range(min(SLOTS, blocks)):
        for copy in weight_copies(j, j):
            copy.start()

    low = dot_nt(tok_ref[...], at_ref[...])
    yb = dot_nt(cot_ref[...], bd_ref[...])
    gd = gates_ref[...]
    rank = bd_ref.shape[0] // 4
    lane = lax.broadcasted_iota(jnp.int32, yb.shape, 1) // rank
    scale = jnp.zeros_like(yb)
    for j in range(4):
        scale = jnp.where(lane == j, gd[:, j : j + 1], scale)
    small[t, row_ds(e), 0:128] = low
    small[t, row_ds(e), 128:256] = jnp.concatenate([yb * scale, gd], axis=1)
    for i in range(1, n):
        start(z_copy(1, i))
    start(x_copy(1, 0))
    start(sib_copy(1, 0))
    for i in range(1, n + 1):
        if i < n:
            for k in range(2):
                landed(k, e, z_from(i), gz_r.at[k, i])
                start(x_copy(k, i))
                start(sib_copy(k, i))
        for k in range(2):
            landed(k, xc, z_from(i - 1), gx_r.at[k, i - 1])
            start(fwd_copy(k, i - 1))
    for i in range(n):
        for k in range(2):
            landed(k, sib, z_from(i), gs_r.at[k, i])
            landed(k, diag, z_from(i), gf_r.at[k, i])

    total = small[0]
    for i in range(1, n):
        total = total + small[i]
    ri = lax.broadcasted_iota(jnp.int32, (256, 128), 0)
    rj = lax.broadcasted_iota(jnp.int32, (256, 128), 1)
    hit = (rj < 32) & (ri == e * 32 + rj)
    hit = hit | ((rj >= 32) & (rj < 48) & (ri == 128 + e * 16 + rj - 32))
    hit = hit | ((rj == 48) & (ri == 192 + e))
    picked = dot_exact(total, hit.astype(F32))
    pj = lax.broadcasted_iota(jnp.int32, picked.shape, 1)
    picked = jnp.where(pj == 48, picked * (1.0 / n), picked)
    sel_ref[...] = picked
    selt_ref[...] = picked.T
    gcol = picked[:, 48:49]
    for q in range(n):
        c = slice(q * f, (q + 1) * f)
        gmat[:, c] = (gcol * xy[1, :, c].astype(F32)).astype(BF)
    acc[...] = jnp.zeros_like(acc)
    tacc[...] = jnp.zeros_like(tacc)

    def body(j, carry):
        slot = lax.rem(j, SLOTS)
        cg, cu, cd = weight_copies(j, slot)
        cg.wait()
        cu.wait()
        cd.wait()
        cols = pl.ds(pl.multiple_of(j * BLOCK, BLOCK), BLOCK)
        bin0, bin1 = bin_ref[0:16, cols], bin_ref[16:32, cols]
        adt = adt_ref[:, cols]
        sel = sel_ref[...]
        l0, l1, qn = sel[:, 0:16].astype(BF), sel[:, 16:32].astype(BF), sel[:, 32:48].astype(BF)
        selt = selt_ref[0:48, :].astype(BF)
        x = xy[0]
        p = dot_nn(x, wg_buf[slot]) + adapter_scale * dot_nn(l0, bin0)
        u = dot_nn(x, wu_buf[slot]) + adapter_scale * dot_nn(l1, bin1)
        ee = dot_nt(gmat[...], wd_buf[slot]) + adapter_scale * dot_nn(qn, adt)
        sig = jax.nn.sigmoid(p)
        silu = p * sig
        h = (silu * u).astype(BF)
        dg = (ee * u * sig * (1.0 + p * (1.0 - sig))).astype(BF)
        du = (ee * silu).astype(BF)
        eout_ref[0:16, cols] = adapter_scale * dot_nn(selt[0:16], dg)
        eout_ref[16:32, cols] = adapter_scale * dot_nn(selt[16:32], du)
        din_ref[:, cols] = adapter_scale * dot_nn(selt[32:48], h)
        tacc[0:16, :] += dot_nt(bin0, dg)
        tacc[16:32, :] += dot_nt(bin1, du)
        tacc[32:48, :] += dot_nt(adt, h)
        for q in range(n):
            c = slice(q * f, (q + 1) * f)
            acc[0, :, c] += dot_nn(h, wd_buf[slot, :, c])
            acc[1, :, c] += dot_nt(dg, wg_buf[slot, c, :]) + dot_nt(du, wu_buf[slot, c, :])

        @pl.when(j + SLOTS < blocks)
        def _():
            for copy in weight_copies(j + SLOTS, slot):
                copy.start()

        return carry

    lax.fori_loop(0, blocks, body, 0)

    def mine(a, o, q):
        v = acc[a, row_ds(o), col_ds(q)]
        return v * sel_ref[row_ds(o), 48:49] if a == 0 else v

    def order(i):
        return z_to(i + 1) if i + 1 < n else t

    for i in range(n):
        q = order(i)
        for a in range(2):
            s1[i, 0, a] = mine(a, diag, q).astype(BF)
            s1[i, 1, a] = mine(a, sib, q).astype(BF)
        start(remote(s1.at[i], r1.at[i], c1_s.at[i], c1_r.at[i], sib, t))
    tacc[32:48, :] = tacc[32:48, :] * selt_ref[48:49, :]
    for i in range(1, n):
        start(remote(tacc, tz.at[i], tz_s.at[i], tz_r.at[i], e, z_to(i)))
    for i in range(n):
        q = order(i)
        remote(s1.at[i], r1.at[i], c1_s.at[i], c1_r.at[i], sib, t).wait_recv()
        for a in range(2):
            s2[i, a] = (mine(a, xc, q) + r1[i, 0, a].astype(F32)).astype(BF)
        start(remote(s2.at[i], r2.at[i], c2_s.at[i], c2_r.at[i], xc, t))
    t_sum = tacc[...]
    for i in range(1, n):
        remote(tacc, tz.at[i], tz_s.at[i], tz_r.at[i], e, z_to(i)).wait_recv()
        t_sum = t_sum + tz[i]
    ts[...] = t_sum
    for j in range(1, 4):
        start(remote(ts, te.at[j], te_s.at[j], te_r.at[j], lax.rem(e + j, 4), t))
    for i in range(n):
        q = order(i)
        remote(s2.at[i], r2.at[i], c2_s.at[i], c2_r.at[i], xc, t).wait_recv()
        for a in range(2):
            v = mine(a, e, q) + r1[i, 1, a].astype(F32) + r2[i, a].astype(F32)
            if i + 1 < n:
                s3[i, a] = v.astype(BF)
            else:
                keep[a] = v
        if i + 1 < n:
            start(remote(s3.at[i], r3.at[i], c3_s.at[i], c3_r.at[i], e, q))

    def place(src, v):
        tvz[pl.ds(pl.multiple_of(src * 32, 32), 32), :] = v[0:32]
        tvz[pl.ds(pl.multiple_of(128 + src * 16, 16), 16), :] = v[32:48]

    place(e, t_sum)
    for j in range(1, 4):
        remote(ts, te.at[j], te_s.at[j], te_r.at[j], lax.rem(e + j, 4), t).wait_recv()
        place(lax.rem(e - j + 4, 4), te[j])
    piece = width // (4 * n)
    cols = pl.ds(pl.multiple_of((e * n + t) * piece, piece), piece)
    ein_ref[...] = adapter_scale * dot_exact(tvz[0:128, :], xy[0, :, cols].astype(F32))
    dout_ref[...] = adapter_scale * dot_exact(tvz[128:192, :], xy[1, :, cols].astype(F32))
    tvzt[...] = tvz[...].T
    own = tvzt[row_ds(e), :]
    add_out = dot_exact(own[:, 128:192], bd_ref[...].astype(F32))
    add_grad = dot_exact(own[:, 0:128], at_ref[...].astype(F32))
    keep[0] = keep[0] + adapter_scale * add_out
    keep[1] = keep[1] + adapter_scale * add_grad
    for i in range(n - 1):
        remote(s3.at[i], r3.at[i], c3_s.at[i], c3_r.at[i], e, z_to(i + 1)).wait_recv()
        for a in range(2):
            keep[a] = keep[a] + r3[i, a].astype(F32)
    mixed_ref[...] = keep[0].astype(BF)
    grad_ref[...] = keep[1].astype(BF)
    for copy in sends:
        copy.wait_send()


def fused(
    tokens, route_experts, route_weight_values, cotangent,
    gate_weight_frozen, up_weight_frozen, down_weight_frozen,
    entry_input_maps, entry_output_maps, down_input_maps, down_output_maps,
):
    n = lax.axis_size("tensor")
    tr, f = tokens.shape
    width, rows = f * n, tr * 4
    units = down_weight_frozen.shape[1]
    labels = jnp.arange(64, dtype=jnp.int32)
    gates = jnp.sum(
        jnp.where(
            route_experts[:, :, None] == labels[None, None, :],
            route_weight_values.astype(F32)[:, :, None],
            0.0,
        ),
        axis=1,
    )
    at = jnp.swapaxes(entry_input_maps, 2, 3).reshape(128, f)
    bd = down_output_maps.reshape(64, f)
    bins = entry_output_maps.reshape(32, units)
    adt = down_input_maps[0].T
    piece = width // (4 * n)
    vm = pl.BlockSpec(memory_space=pltpu.VMEM)
    anym = pl.BlockSpec(memory_space=pl.ANY)
    sds = jax.ShapeDtypeStruct
    dma = pltpu.SemaphoreType.DMA
    mixed, grad, ein, eout, din, dout = pl.pallas_call(
        functools.partial(fused_kernel, n),
        out_shape=(
            sds((tr, f), BF), sds((tr, f), BF), sds((128, piece), F32),
            sds((32, units), F32), sds((16, units), F32), sds((64, piece), F32),
        ),
        in_specs=[vm] * 7 + [anym] * 3,
        out_specs=(vm,) * 6,
        scratch_shapes=[
            pltpu.VMEM((2, rows, width), BF),
            pltpu.VMEM((n, rows, 256), F32),
            pltpu.VMEM((rows, width), BF),
            pltpu.VMEM((rows, 128), F32),
            pltpu.VMEM((128, rows), F32),
            pltpu.VMEM((2, rows, width), F32),
            pltpu.VMEM((48, rows), F32),
            pltpu.VMEM((n, 48, rows), F32),
            pltpu.VMEM((48, rows), F32),
            pltpu.VMEM((4, 48, rows), F32),
            pltpu.VMEM((192, rows), F32),
            pltpu.VMEM((rows, 192), F32),
            pltpu.VMEM((SLOTS, width, BLOCK), BF),
            pltpu.VMEM((SLOTS, width, BLOCK), BF),
            pltpu.VMEM((SLOTS, BLOCK, width), BF),
            pltpu.VMEM((n, 2, 2, tr, f), BF),
            pltpu.VMEM((n, 2, 2, tr, f), BF),
            pltpu.VMEM((n, 2, tr, f), BF),
            pltpu.VMEM((n, 2, tr, f), BF),
            pltpu.VMEM((n - 1, 2, tr, f), BF),
            pltpu.VMEM((n - 1, 2, tr, f), BF),
            pltpu.VMEM((2, tr, f), F32),
            dma((3, SLOTS)),
        ]
        + [dma((2, n))] * 8
        + [dma((n,))] * 2 + [dma((4,))] * 2 + [dma((n,))] * 6,
        compiler_params=pltpu.CompilerParams(
            collective_id=0, has_side_effects=True, vmem_limit_bytes=63 * 2**20
        ),
        cost_estimate=pl.CostEstimate(
            flops=12 * rows * width * units, bytes_accessed=6 * width * units, transcendentals=0
        ),
    )(tokens, cotangent, gates, at, bd, bins, adt,
      gate_weight_frozen, up_weight_frozen, down_weight_frozen)
    ein = jnp.swapaxes(ein.reshape(4, 2, 16, piece), 2, 3)
    return (
        mixed, grad, ein, eout.reshape(1, 2, 16, units), din.T[None],
        dout.reshape(4, 16, piece),
    )


def fits(mesh):
    return mesh.shape["expert"] == 4 and mesh.shape["tensor"] == 4


def solution(mesh):
    in_specs = (
        P(("group", "expert"), "tensor"),
        P(("group", "expert"), None),
        P(("group", "expert"), None),
        P(("group", "expert"), "tensor"),
        P("expert", None, "tensor"),
        P("expert", None, "tensor"),
        P("expert", "tensor", None),
        P("group", None, "tensor", None),
        P(("group", "expert"), None, None, "tensor"),
        P(("group", "expert"), "tensor", None),
        P("group", None, "tensor"),
    )
    out_specs = (
        P(("group", "expert"), "tensor"),
        P(("group", "expert"), "tensor"),
        P("group", None, ("expert", "tensor"), None),
        P(("group", "expert"), None, None, "tensor"),
        P(("group", "expert"), "tensor", None),
        P("group", None, ("expert", "tensor")),
    )
    step = fused if fits(mesh) else local
    return jax.shard_map(step, mesh=mesh, in_specs=in_specs, out_specs=out_specs, check_vma=False)
```

```python
import functools

import jax
import jax.numpy as jnp
from jax import lax
from jax.experimental import pallas as pl
from jax.experimental.pallas import tpu as pltpu
from jax.sharding import PartitionSpec as P

MOST = 20


adapter_scale = 2.0
exact_precision = lax.Precision.HIGHEST


def expert_forward_step(
    expert_token_rows,
    expert_gradient_rows,
    expert_gate_values,
    gate_weight_slices,
    up_weight_slices,
    down_weight_slices,
    adapter_a_in,
    entry_adapter_outmaps,
    down_adapter_inmaps,
    adapter_b_down,
):
    narrow_gate = jnp.dot(
        expert_token_rows, adapter_a_in[0], preferred_element_type=jnp.float32
    ).astype(jnp.bfloat16)
    narrow_up = jnp.dot(
        expert_token_rows, adapter_a_in[1], preferred_element_type=jnp.float32
    ).astype(jnp.bfloat16)
    gate_preactivation = jnp.dot(
        expert_token_rows, gate_weight_slices, preferred_element_type=jnp.float32
    ) + adapter_scale * jnp.dot(
        narrow_gate, entry_adapter_outmaps[0], preferred_element_type=jnp.float32
    )
    up_preactivation = jnp.dot(
        expert_token_rows, up_weight_slices, preferred_element_type=jnp.float32
    ) + adapter_scale * jnp.dot(
        narrow_up, entry_adapter_outmaps[1], preferred_element_type=jnp.float32
    )
    sigmoid_gate = jax.nn.sigmoid(gate_preactivation)
    silu_gate = gate_preactivation * sigmoid_gate
    hidden_state = (silu_gate * up_preactivation).astype(jnp.bfloat16)
    narrow_down = jnp.dot(hidden_state, down_adapter_inmaps, preferred_element_type=jnp.float32)
    down_output_maps_spread = adapter_b_down.astype(jnp.float32)
    expert_output_rows = jnp.dot(
        hidden_state, down_weight_slices, preferred_element_type=jnp.float32
    ) + adapter_scale * jnp.dot(narrow_down, down_output_maps_spread, precision=exact_precision)
    weighted = expert_gate_values * expert_output_rows
    output_gradient = (expert_gate_values * expert_gradient_rows.astype(jnp.float32)).astype(
        jnp.bfloat16
    )
    narrow_gradient = jnp.dot(output_gradient, adapter_b_down.T, preferred_element_type=jnp.float32)
    hidden_gradient = jnp.dot(
        output_gradient, down_weight_slices.T, preferred_element_type=jnp.float32
    ) + adapter_scale * jnp.dot(
        narrow_gradient, down_adapter_inmaps.astype(jnp.float32).T, precision=exact_precision
    )
    down_inmaps_gradient = adapter_scale * jnp.dot(
        hidden_state.astype(jnp.float32).T, narrow_gradient, precision=exact_precision
    )
    down_outmaps_gradient = adapter_scale * jnp.dot(
        narrow_down.T, output_gradient.astype(jnp.float32), precision=exact_precision
    )
    gate_gradient = (
        hidden_gradient
        * up_preactivation
        * sigmoid_gate
        * (1.0 + gate_preactivation * (1.0 - sigmoid_gate))
    ).astype(jnp.bfloat16)
    up_gradient = (hidden_gradient * silu_gate).astype(jnp.bfloat16)
    reverse_gate_step = jnp.dot(
        gate_gradient, entry_adapter_outmaps[0].T, preferred_element_type=jnp.float32
    )
    reverse_up_step = jnp.dot(
        up_gradient, entry_adapter_outmaps[1].T, preferred_element_type=jnp.float32
    )
    entry_outmaps_gradient = adapter_scale * jnp.stack(
        [
            jnp.dot(narrow_gate.T, gate_gradient, preferred_element_type=jnp.float32),
            jnp.dot(narrow_up.T, up_gradient, preferred_element_type=jnp.float32),
        ]
    )
    token_rows_spread = expert_token_rows.astype(jnp.float32)
    entry_inmaps_gradient = adapter_scale * jnp.stack(
        [
            jnp.dot(token_rows_spread.T, reverse_gate_step, precision=exact_precision),
            jnp.dot(token_rows_spread.T, reverse_up_step, precision=exact_precision),
        ]
    )
    entry_input_maps_spread = adapter_a_in.astype(jnp.float32)
    input_gradient = jnp.dot(
        gate_gradient, gate_weight_slices.T, preferred_element_type=jnp.float32
    ) + jnp.dot(up_gradient, up_weight_slices.T, preferred_element_type=jnp.float32)
    input_gradient = input_gradient + adapter_scale * (
        jnp.dot(reverse_gate_step, entry_input_maps_spread[0].T, precision=exact_precision)
        + jnp.dot(reverse_up_step, entry_input_maps_spread[1].T, precision=exact_precision)
    )
    return (
        weighted,
        input_gradient,
        entry_inmaps_gradient,
        entry_outmaps_gradient,
        down_inmaps_gradient,
        down_outmaps_gradient,
    )


def route_positions(route_experts, expert_number):
    flat_ids = route_experts.reshape(-1)
    expert_labels = jnp.arange(expert_number, dtype=jnp.int32)
    one_hot = (flat_ids[:, None] == expert_labels[None, :]).astype(jnp.int32)
    earlier = jnp.cumsum(one_hot, axis=0) - one_hot
    return jnp.sum(earlier * one_hot, axis=1)


def spread_slots(rows, expert_number, capacity, copy_count):
    return jnp.repeat(rows.reshape((expert_number, capacity) + rows.shape[1:]), copy_count, axis=0)


def collect_rows(back, token_hits, expert_number, copy_count, capacity):
    row_width = back.shape[2]
    merged = jnp.sum(back.reshape(expert_number, copy_count, capacity, row_width), axis=1).reshape(
        expert_number * capacity, row_width
    )
    return jnp.dot(token_hits.T, merged, precision=exact_precision)


def local(
    tokens,
    route_experts,
    route_weight_values,
    cotangent,
    gate_weight_frozen,
    up_weight_frozen,
    down_weight_frozen,
    entry_input_maps,
    entry_output_maps,
    down_input_maps,
    down_output_maps,
):
    tok_rows = tokens.shape[0]
    expert_number = entry_input_maps.shape[0]
    adapter_rank_count = entry_input_maps.shape[3]
    route_count = route_experts.shape[1]
    owner_count = lax.axis_size("expert")
    tensor_count = lax.axis_size("tensor")
    model_width = tokens.shape[1] * tensor_count
    copy_count = owner_count // expert_number
    capacity = MOST
    flat_ids = route_experts.reshape(-1)
    position = route_positions(route_experts, expert_number)
    slot_of = flat_ids * capacity + position
    slot_ids = jnp.arange(expert_number * capacity, dtype=jnp.int32)
    chosen = slot_ids[:, None] == slot_of[None, :]
    pick_route = chosen.astype(jnp.bfloat16)
    hit_counts = jnp.sum(
        chosen.reshape(expert_number * capacity, tok_rows, route_count).astype(jnp.int32), axis=2
    )
    pick_token = hit_counts.astype(jnp.bfloat16)
    token_hits = hit_counts.astype(jnp.float32)
    send_gates = jnp.dot(
        pick_route, route_weight_values.reshape(-1), preferred_element_type=jnp.float32
    ).astype(jnp.bfloat16)
    send_gates = spread_slots(send_gates, expert_number, capacity, copy_count)
    full_tokens, full_grads = (
        lax.all_gather(tokens, "tensor", axis=1, tiled=True),
        lax.all_gather(cotangent, "tensor", axis=1, tiled=True),
    )
    send_tokens = spread_slots(
        jnp.dot(pick_token, full_tokens, preferred_element_type=jnp.float32).astype(jnp.bfloat16),
        expert_number,
        capacity,
        copy_count,
    )
    send_grads = spread_slots(
        jnp.dot(pick_token, full_grads, preferred_element_type=jnp.float32).astype(jnp.bfloat16),
        expert_number,
        capacity,
        copy_count,
    )
    got_tokens, got_grads, got_gates = (
        lax.all_to_all(send_tokens, "expert", split_axis=0, concat_axis=0, tiled=True),
        lax.all_to_all(send_grads, "expert", split_axis=0, concat_axis=0, tiled=True),
        lax.all_to_all(send_gates, "expert", split_axis=0, concat_axis=0, tiled=True),
    )
    holder_index = lax.axis_index("expert") // copy_count
    entry_input_maps_local = lax.dynamic_index_in_dim(
        entry_input_maps, holder_index, 0, keepdims=False
    )
    down_output_maps_local = lax.dynamic_index_in_dim(
        down_output_maps, holder_index, 0, keepdims=False
    )
    a_in_full, b_down_full = (
        lax.all_gather(entry_input_maps_local, "tensor", axis=1, tiled=True),
        lax.all_gather(down_output_maps_local, "tensor", axis=1, tiled=True),
    )
    expert_token_rows = got_tokens.reshape(-1, model_width)
    expert_gradient_rows = got_grads.reshape(-1, model_width)
    expert_gate_values = got_gates.reshape(-1).astype(jnp.float32)[:, None]
    step_results = expert_forward_step(
        expert_token_rows,
        expert_gradient_rows,
        expert_gate_values,
        gate_weight_frozen[0],
        up_weight_frozen[0],
        down_weight_frozen[0],
        a_in_full,
        entry_output_maps[0],
        down_input_maps[0],
        b_down_full,
    )
    (
        weighted,
        input_gradient,
        entry_inmaps_gradient,
        entry_outmaps_gradient,
        down_inmaps_gradient,
        down_outmaps_gradient,
    ) = step_results
    weighted = weighted.reshape(owner_count, capacity, model_width)
    input_gradient = input_gradient.reshape(owner_count, capacity, model_width)
    back_out, back_grad = (
        lax.all_to_all(weighted, "expert", split_axis=0, concat_axis=0, tiled=True),
        lax.all_to_all(input_gradient, "expert", split_axis=0, concat_axis=0, tiled=True),
    )
    token_out = collect_rows(back_out, token_hits, expert_number, copy_count, capacity)
    token_grad = collect_rows(back_grad, token_hits, expert_number, copy_count, capacity)
    total_out, total_grad = (
        lax.psum_scatter(token_out, "tensor", scatter_dimension=1, tiled=True),
        lax.psum_scatter(token_grad, "tensor", scatter_dimension=1, tiled=True),
    )
    table_a_in = jnp.zeros((expert_number, 2, model_width, adapter_rank_count), jnp.float32)
    table_a_in = lax.dynamic_update_index_in_dim(table_a_in, entry_inmaps_gradient, holder_index, 0)
    table_b_down = jnp.zeros((expert_number, adapter_rank_count, model_width), jnp.float32)
    table_b_down = lax.dynamic_update_index_in_dim(
        table_b_down, down_outmaps_gradient, holder_index, 0
    )
    summed_a_in, summed_b_down = (
        lax.psum_scatter(table_a_in, ("expert", "tensor"), scatter_dimension=2, tiled=True),
        lax.psum_scatter(table_b_down, ("expert", "tensor"), scatter_dimension=2, tiled=True),
    )
    return (
        total_out.astype(jnp.bfloat16),
        total_grad.astype(jnp.bfloat16),
        summed_a_in,
        entry_outmaps_gradient[None],
        down_inmaps_gradient[None],
        summed_b_down,
    )


BF = jnp.bfloat16
F32 = jnp.float32
MESH = pl.DeviceIdType.MESH
BLOCK = 256
SLOTS = 4


def dot_nn(a, b):
    return jnp.dot(a, b, preferred_element_type=F32)


def dot_nt(a, b):
    return lax.dot_general(a, b, (((1,), (1,)), ((), ())), preferred_element_type=F32)


def dot_exact(a, b):
    return jnp.dot(a, b, preferred_element_type=F32, precision=exact_precision)


def fused_kernel(
    n_tensor,
    tok_ref, cot_ref, route_ref, weight_ref, at_ref, bd_ref, bin_ref, adt_ref, wg_ref, wu_ref, wd_ref,
    mixed_ref, grad_ref, ein_ref, eout_ref, din_ref, dout_ref,
    xy, small, gmat, sel_ref, selt_ref, acc, acct, tacc, tz, ts, te, tvz, tvzt,
    wg_buf, wu_buf, wd_buf, s1, r1, s2, r2, s3, r3, keep,
    wsem, gz_s, gz_r, gx_s, gx_r, gs_s, gs_r, gf_s, gf_r,
    tz_s, tz_r, te_s, te_r, c1_s, c1_r, c2_s, c2_r, c3_s, c3_r,
):
    e = lax.axis_index("expert")
    t = lax.axis_index("tensor")
    n = n_tensor
    tr, f = tok_ref.shape
    width, rows = gmat.shape
    units = adt_ref.shape[1]
    blocks = units // BLOCK
    xi, ci = e // 2, e % 2
    sib = 2 * xi + (1 - ci)
    xc = 2 * (1 - xi) + ci
    diag = 2 * (1 - xi) + (1 - ci)

    def z_to(i):
        return lax.rem(t + i, n)

    def z_from(i):
        return lax.rem(t - i + n, n)

    def remote(src, dst, ss, rs, pe, pt):
        return pltpu.make_async_remote_copy(
            src_ref=src, dst_ref=dst, send_sem=ss, recv_sem=rs,
            device_id={"expert": pe, "tensor": pt}, device_id_type=MESH,
        )

    def weight_copies(j, slot):
        cols = pl.ds(pl.multiple_of(j * BLOCK, BLOCK), BLOCK)
        return (
            pltpu.make_async_copy(wg_ref.at[0, :, cols], wg_buf.at[slot], wsem.at[0, slot]),
            pltpu.make_async_copy(wu_ref.at[0, :, cols], wu_buf.at[slot], wsem.at[1, slot]),
            pltpu.make_async_copy(wd_ref.at[0, cols, :], wd_buf.at[slot], wsem.at[2, slot]),
        )

    barrier = pltpu.get_barrier_semaphore()
    for i in range(1, n):
        pl.semaphore_signal(
            barrier, inc=1, device_id={"expert": e, "tensor": z_to(i)}, device_id_type=MESH
        )
    for j in range(1, 4):
        pl.semaphore_signal(
            barrier, inc=1, device_id={"expert": lax.rem(e + j, 4), "tensor": t},
            device_id_type=MESH,
        )

    def row_ds(o):
        return pl.ds(pl.multiple_of(o * tr, tr), tr)

    def col_ds(q):
        return pl.ds(pl.multiple_of(q * f, f), f)

    def part(k, oe, ot):
        if k == 0:
            return xy.at[:, row_ds(oe), col_ds(ot)]
        return small.at[ot, row_ds(oe), :]

    xy[0, row_ds(e), col_ds(t)] = tok_ref[...]
    xy[1, row_ds(e), col_ds(t)] = cot_ref[...]
    pl.semaphore_wait(barrier, n - 1 + 3)

    sends = []

    def start(copy):
        copy.start()
        sends.append(copy)

    def z_copy(k, i):
        return remote(part(k, e, t), part(k, e, t), gz_s.at[k, i], gz_r.at[k, i], e, z_to(i))

    def x_copy(k, i):
        b = part(k, e, z_from(i))
        return remote(b, b, gx_s.at[k, i], gx_r.at[k, i], xc, t)

    def sib_copy(k, i):
        b = part(k, e, z_from(i))
        return remote(b, b, gs_s.at[k, i], gs_r.at[k, i], sib, t)

    def fwd_copy(k, i):
        b = part(k, xc, z_from(i))
        return remote(b, b, gf_s.at[k, i], gf_r.at[k, i], sib, t)

    def landed(k, oe, ot, rs):
        b = part(k, oe, ot)
        remote(b, b, rs, rs, sib, t).wait_recv()

    for i in range(1, n):
        start(z_copy(0, i))
    start(x_copy(0, 0))
    start(sib_copy(0, 0))
    for j in range(min(SLOTS, blocks)):
        for copy in weight_copies(j, j):
            copy.start()

    low = dot_nt(tok_ref[...], at_ref[...])
    yb = dot_nt(cot_ref[...], bd_ref[...])
    label = lax.broadcasted_iota(jnp.int32, (tr, 64), 1)
    routes, weights = route_ref[...], weight_ref[...].astype(F32)
    gd = jnp.zeros((tr, 64), F32)
    for j in range(routes.shape[1]):
        gd = gd + jnp.where(label == routes[:, j : j + 1], weights[:, j : j + 1], 0.0)
    rank = bd_ref.shape[0] // 4
    lane = lax.broadcasted_iota(jnp.int32, yb.shape, 1) // rank
    scale = jnp.zeros_like(yb)
    for j in range(4):
        scale = jnp.where(lane == j, gd[:, j : j + 1], scale)
    small[t, row_ds(e), 0:128] = low
    small[t, row_ds(e), 128:256] = jnp.concatenate([yb * scale, gd], axis=1)
    for i in range(1, n):
        start(z_copy(1, i))
    start(x_copy(1, 0))
    start(sib_copy(1, 0))
    for i in range(1, n + 1):
        if i < n:
            for k in range(2):
                landed(k, e, z_from(i), gz_r.at[k, i])
                start(x_copy(k, i))
                start(sib_copy(k, i))
        for k in range(2):
            landed(k, xc, z_from(i - 1), gx_r.at[k, i - 1])
            start(fwd_copy(k, i - 1))
    for i in range(n):
        for k in range(2):
            landed(k, sib, z_from(i), gs_r.at[k, i])
            landed(k, diag, z_from(i), gf_r.at[k, i])

    total = small[0]
    for i in range(1, n):
        total = total + small[i]
    ri = lax.broadcasted_iota(jnp.int32, (256, 128), 0)
    rj = lax.broadcasted_iota(jnp.int32, (256, 128), 1)
    hit = (rj < 32) & (ri == e * 32 + rj)
    hit = hit | ((rj >= 32) & (rj < 48) & (ri == 128 + e * 16 + rj - 32))
    hit = hit | ((rj == 48) & (ri == 192 + e))
    picked = dot_exact(total, hit.astype(F32))
    pj = lax.broadcasted_iota(jnp.int32, picked.shape, 1)
    picked = jnp.where(pj == 48, picked * (1.0 / n), picked)
    sel_ref[...] = picked
    selt_ref[...] = picked.T
    gcol = picked[:, 48:49]
    for q in range(n):
        c = slice(q * f, (q + 1) * f)
        gmat[c, :] = (gcol * xy[1, :, c].astype(F32)).T.astype(BF)
    acc[0] = jnp.zeros_like(acc[0])
    acct[...] = jnp.zeros_like(acct)
    tacc[...] = jnp.zeros_like(tacc)

    def body(j, carry):
        slot = lax.rem(j, SLOTS)
        cg, cu, cd = weight_copies(j, slot)
        cg.wait()
        cu.wait()
        cd.wait()
        cols = pl.ds(pl.multiple_of(j * BLOCK, BLOCK), BLOCK)
        bin0, bin1 = bin_ref[0:16, cols], bin_ref[16:32, cols]
        adt = adt_ref[:, cols]
        sel = sel_ref[...]
        l0, l1, qn = sel[:, 0:16].astype(BF), sel[:, 16:32].astype(BF), sel[:, 32:48].astype(BF)
        selt = selt_ref[0:48, :].astype(BF)
        x = xy[0]
        p = dot_nn(x, wg_buf[slot]) + adapter_scale * dot_nn(l0, bin0)
        u = dot_nn(x, wu_buf[slot]) + adapter_scale * dot_nn(l1, bin1)
        ee = dot_nn(wd_buf[slot], gmat[...]).T + adapter_scale * dot_nn(qn, adt)
        sig = jax.nn.sigmoid(p)
        silu = p * sig
        h = (silu * u).astype(BF)
        dgf = ee * u * sig * (1.0 + p * (1.0 - sig))
        duf = ee * silu
        dg, du = dgf.astype(BF), duf.astype(BF)
        dgt, dut = dgf.T.astype(BF), duf.T.astype(BF)
        eout_ref[0:16, cols] = adapter_scale * dot_nn(selt[0:16], dg)
        eout_ref[16:32, cols] = adapter_scale * dot_nn(selt[16:32], du)
        din_ref[:, cols] = adapter_scale * dot_nn(selt[32:48], h)
        tacc[0:16, :] += dot_nt(bin0, dg)
        tacc[16:32, :] += dot_nt(bin1, du)
        tacc[32:48, :] += dot_nt(adt, h)
        for q in range(n):
            c = slice(q * f, (q + 1) * f)
            acc[0, :, c] += dot_nn(h, wd_buf[slot, :, c])
            acct[c, :] += dot_nn(wg_buf[slot, c, :], dgt) + dot_nn(wu_buf[slot, c, :], dut)

        @pl.when(j + SLOTS < blocks)
        def _():
            for copy in weight_copies(j + SLOTS, slot):
                copy.start()

        return carry

    lax.fori_loop(0, blocks, body, 0)
    for q in range(n):
        c = slice(q * f, (q + 1) * f)
        acc[1, :, c] = acct[c, :].T

    def mine(a, o, q):
        v = acc[a, row_ds(o), col_ds(q)]
        return v * sel_ref[row_ds(o), 48:49] if a == 0 else v

    def order(i):
        return z_to(i + 1) if i + 1 < n else t

    for i in range(n):
        q = order(i)
        for a in range(2):
            s1[i, 0, a] = mine(a, diag, q).astype(BF)
            s1[i, 1, a] = mine(a, sib, q).astype(BF)
        start(remote(s1.at[i], r1.at[i], c1_s.at[i], c1_r.at[i], sib, t))
    tacc[32:48, :] = tacc[32:48, :] * selt_ref[48:49, :]
    for i in range(1, n):
        start(remote(tacc, tz.at[i], tz_s.at[i], tz_r.at[i], e, z_to(i)))
    for i in range(n):
        q = order(i)
        remote(s1.at[i], r1.at[i], c1_s.at[i], c1_r.at[i], sib, t).wait_recv()
        for a in range(2):
            s2[i, a] = (mine(a, xc, q) + r1[i, 0, a].astype(F32)).astype(BF)
        start(remote(s2.at[i], r2.at[i], c2_s.at[i], c2_r.at[i], xc, t))
    t_sum = tacc[...]
    for i in range(1, n):
        remote(tacc, tz.at[i], tz_s.at[i], tz_r.at[i], e, z_to(i)).wait_recv()
        t_sum = t_sum + tz[i]
    ts[...] = t_sum
    for j in range(1, 4):
        start(remote(ts, te.at[j], te_s.at[j], te_r.at[j], lax.rem(e + j, 4), t))
    for i in range(n):
        q = order(i)
        remote(s2.at[i], r2.at[i], c2_s.at[i], c2_r.at[i], xc, t).wait_recv()
        for a in range(2):
            v = mine(a, e, q) + r1[i, 1, a].astype(F32) + r2[i, a].astype(F32)
            if i + 1 < n:
                s3[i, a] = v.astype(BF)
            else:
                keep[a] = v
        if i + 1 < n:
            start(remote(s3.at[i], r3.at[i], c3_s.at[i], c3_r.at[i], e, q))

    def place(src, v):
        tvz[pl.ds(pl.multiple_of(src * 32, 32), 32), :] = v[0:32]
        tvz[pl.ds(pl.multiple_of(128 + src * 16, 16), 16), :] = v[32:48]

    place(e, t_sum)
    for j in range(1, 4):
        remote(ts, te.at[j], te_s.at[j], te_r.at[j], lax.rem(e + j, 4), t).wait_recv()
        place(lax.rem(e - j + 4, 4), te[j])
    piece = width // (4 * n)
    cols = pl.ds(pl.multiple_of((e * n + t) * piece, piece), piece)
    ein_ref[...] = adapter_scale * dot_exact(tvz[0:128, :], xy[0, :, cols].astype(F32))
    dout_ref[...] = adapter_scale * dot_exact(tvz[128:192, :], xy[1, :, cols].astype(F32))
    tvzt[...] = tvz[...].T
    own = tvzt[row_ds(e), :]
    add_out = dot_exact(own[:, 128:192], bd_ref[...].astype(F32))
    add_grad = dot_exact(own[:, 0:128], at_ref[...].astype(F32))
    keep[0] = keep[0] + adapter_scale * add_out
    keep[1] = keep[1] + adapter_scale * add_grad
    for i in range(n - 1):
        remote(s3.at[i], r3.at[i], c3_s.at[i], c3_r.at[i], e, z_to(i + 1)).wait_recv()
        for a in range(2):
            keep[a] = keep[a] + r3[i, a].astype(F32)
    mixed_ref[...] = keep[0].astype(BF)
    grad_ref[...] = keep[1].astype(BF)
    for copy in sends:
        copy.wait_send()


def store_results(*refs):
    for source, target in zip(refs[:6], refs[6:]):
        target[...] = source[...]


def fused(
    tokens, route_experts, route_weight_values, cotangent,
    gate_weight_frozen, up_weight_frozen, down_weight_frozen,
    entry_input_maps, entry_output_maps, down_input_maps, down_output_maps,
):
    n = lax.axis_size("tensor")
    tr, f = tokens.shape
    width, rows = f * n, tr * 4
    units = down_weight_frozen.shape[1]
    at = jnp.swapaxes(entry_input_maps, 2, 3).reshape(128, f)
    bd = down_output_maps.reshape(64, f)
    bins = entry_output_maps.reshape(32, units)
    adt = down_input_maps[0].T
    piece = width // (4 * n)
    vm = pl.BlockSpec(memory_space=pltpu.VMEM)
    anym = pl.BlockSpec(memory_space=pl.ANY)
    sds = jax.ShapeDtypeStruct
    dma = pltpu.SemaphoreType.DMA
    shapes = (
            sds((tr, f), BF), sds((tr, f), BF), sds((128, piece), F32),
            sds((32, units), F32), sds((16, units), F32), sds((64, piece), F32),
    )
    results = pl.pallas_call(
        functools.partial(fused_kernel, n),
        out_shape=shapes,
        in_specs=[vm] * 8 + [anym] * 3,
        out_specs=(vm,) * 6,
        scratch_shapes=[
            pltpu.VMEM((2, rows, width), BF),
            pltpu.VMEM((n, rows, 256), F32),
            pltpu.VMEM((width, rows), BF),
            pltpu.VMEM((rows, 128), F32),
            pltpu.VMEM((128, rows), F32),
            pltpu.VMEM((2, rows, width), F32),
            pltpu.VMEM((width, rows), F32),
            pltpu.VMEM((48, rows), F32),
            pltpu.VMEM((n, 48, rows), F32),
            pltpu.VMEM((48, rows), F32),
            pltpu.VMEM((4, 48, rows), F32),
            pltpu.VMEM((192, rows), F32),
            pltpu.VMEM((rows, 192), F32),
            pltpu.VMEM((SLOTS, width, BLOCK), BF),
            pltpu.VMEM((SLOTS, width, BLOCK), BF),
            pltpu.VMEM((SLOTS, BLOCK, width), BF),
            pltpu.VMEM((n, 2, 2, tr, f), BF),
            pltpu.VMEM((n, 2, 2, tr, f), BF),
            pltpu.VMEM((n, 2, tr, f), BF),
            pltpu.VMEM((n, 2, tr, f), BF),
            pltpu.VMEM((n - 1, 2, tr, f), BF),
            pltpu.VMEM((n - 1, 2, tr, f), BF),
            pltpu.VMEM((2, tr, f), F32),
            dma((3, SLOTS)),
        ]
        + [dma((2, n))] * 8
        + [dma((n,))] * 2 + [dma((4,))] * 2 + [dma((n,))] * 6,
        compiler_params=pltpu.CompilerParams(
            collective_id=0, has_side_effects=True, vmem_limit_bytes=63 * 2**20
        ),
        cost_estimate=pl.CostEstimate(
            flops=12 * rows * width * units, bytes_accessed=6 * width * units, transcendentals=0
        ),
    )(tokens, cotangent, route_experts, route_weight_values, at, bd, bins, adt,
      gate_weight_frozen, up_weight_frozen, down_weight_frozen)
    mixed, grad, ein, eout, din, dout = pl.pallas_call(
        store_results, out_shape=shapes, in_specs=[vm] * 6, out_specs=(vm,) * 6
    )(*results)
    ein = jnp.swapaxes(ein.reshape(4, 2, 16, piece), 2, 3)
    return (
        mixed, grad, ein, eout.reshape(1, 2, 16, units), din.T[None],
        dout.reshape(4, 16, piece),
    )


def fits(mesh):
    return mesh.shape["expert"] == 4 and mesh.shape["tensor"] == 4


def solution(mesh):
    in_specs = (
        P(("group", "expert"), "tensor"),
        P(("group", "expert"), None),
        P(("group", "expert"), None),
        P(("group", "expert"), "tensor"),
        P("expert", None, "tensor"),
        P("expert", None, "tensor"),
        P("expert", "tensor", None),
        P("group", None, "tensor", None),
        P(("group", "expert"), None, None, "tensor"),
        P(("group", "expert"), "tensor", None),
        P("group", None, "tensor"),
    )
    out_specs = (
        P(("group", "expert"), "tensor"),
        P(("group", "expert"), "tensor"),
        P("group", None, ("expert", "tensor"), None),
        P(("group", "expert"), None, None, "tensor"),
        P(("group", "expert"), "tensor", None),
        P("group", None, ("expert", "tensor")),
    )
    step = fused if fits(mesh) else local
    return jax.shard_map(step, mesh=mesh, in_specs=in_specs, out_specs=out_specs, check_vma=False)
```
